128 devices in a mesh: crow: 16 (over z, x), ccol: 8 (over y, core).
Axes of the slice: x: 4, y: 4, z: 4, core: 2. Of those that a mesh axis runs over, the one named last changes fastest.
Arguments:
- sketch: float32 [524288, 512], P(('crow', 'ccol')), may hold values from -120 to 120, as said below
Outputs:
- posterior_basis: float32 [524288, 512], P(('crow', 'ccol'))
- mean_log_eigen: float32 [], replicated
The draws below stay inside these ranges and needn't reach their ends.
Inputs may be any that keep to these rules, and one draw needn't show every extreme that they name: Entries of the sketch are real numbers of either sign.
All inputs are finite; a program needn't handle non-finite values.
Results may differ from the reference program's by a relative error of at most 0.0003.
Values sent between devices are 32-bit elements; how exact they have to be, the bound alone decides.
A program may use at most 128 MiB of HBM per device.

```python
import math
import jax
import jax.numpy as jnp
from jax import lax

K = 512
ROWS = 524288


def draw_sketch(key, part):
    key = jax.random.fold_in(key, 7)
    keys = jax.random.split(key, 3)
    noise = jnp.clip(jax.random.normal(keys[0], (ROWS, K), jnp.float32), -5.0, 5.0)
    mixed = noise + 0.7 * jnp.roll(noise, 1, axis=1)
    rough = jnp.exp(jax.random.uniform(keys[1], (ROWS, 1), jnp.float32, math.log(0.7), math.log(1.4)))
    mixed = mixed * rough
    ramp = jnp.exp(math.log(3.0) * jnp.arange(ROWS, dtype=jnp.float32)[:, None] / jnp.float32(ROWS - 1))
    column = jnp.exp(jax.random.uniform(keys[2], (1, K), jnp.float32, math.log(0.3), math.log(3.0)))
    return jnp.clip(mixed * ramp * column, -120.0, 120.0).astype(jnp.float32)


def setup_inputs(seed: int = 0) -> dict:
    seeds = jax.random.split(jax.random.key(seed), 2)
    return {
        "sketch": draw_sketch(jax.random.fold_in(seeds[1], 71), 0),
    }


def reference(sketch):
    gram = lax.dot_general(sketch.astype(jnp.float32), sketch.astype(jnp.float32), (((0,), (0,)), ((), ())), precision=lax.Precision.HIGHEST, preferred_element_type=jnp.float32)
    eye = jnp.eye(K, dtype=jnp.float32)
    precision = eye + gram / jnp.float32(ROWS)
    inverse = jnp.linalg.solve(precision, eye)
    inverse = 0.5 * (inverse + inverse.T)
    posterior_basis = jnp.dot(sketch.astype(jnp.float32), inverse.astype(jnp.float32), precision=lax.Precision.HIGHEST, preferred_element_type=jnp.float32)
    logdet = jnp.linalg.slogdet(precision)[1]
    return (posterior_basis, (logdet / jnp.float32(K)).astype(jnp.float32))
```

```python
import functools

import jax
import jax.numpy as jnp
from jax import lax
from jax.experimental import pallas as pl
from jax.experimental.pallas import tpu as pltpu
from jax.sharding import PartitionSpec as P

MESH = pl.DeviceIdType.MESH
F32, BF16 = jnp.float32, jnp.bfloat16
VMEM_LIMIT = 60 * 2**20
CHUNK = 512
GROUP = 16


def split(x):
    high = x.astype(BF16)
    return high, (x - high.astype(F32)).astype(BF16)


def place():
    crow, ccol = lax.axis_index("crow"), lax.axis_index("ccol")
    return crow // 4, crow % 4, ccol // 2, ccol % 2


def peer(here, offset):
    z, x, y, core = here
    dz, dx, dy = offset
    return (((z + dz) % 4) * 4 + (x + dx) % 4, ((y + dy) % 4) * 2 + core)


def hops(offset):
    return sum(min(d, 4 - d) for d in offset)


OFFSETS = sorted(
    [(dz, dx, dy) for dz in range(4) for dx in range(4) for dy in range(4) if (dz, dx, dy) != (0, 0, 0)],
    key=lambda o: (-hops(o), o),
)


def gram_kernel(x_hbm, out, xb, acc, cross, part, crecv, mine, rbuf, load_sem, core_sem, rs_sem, ag_sem, fw_sem):
    rows = x_hbm.shape[0]
    n = rows // CHUNK
    loads = [
        pltpu.make_async_copy(x_hbm.at[pl.ds(i * CHUNK, CHUNK)], xb.at[pl.ds(i * CHUNK, CHUNK)], load_sem.at[i])
        for i in range(n)
    ]
    for load in loads:
        load.start()

    here = place()
    z, x, y, core = here
    chip = (z * 4 + x) * 4 + y
    crow, ccol = lax.axis_index("crow"), lax.axis_index("ccol")
    twin = (crow, ccol + 1 - 2 * core)
    barrier = pltpu.get_barrier_semaphore()
    pl.semaphore_signal(barrier, inc=1, device_id=twin, device_id_type=MESH)
    for offset in OFFSETS:
        pl.semaphore_signal(barrier, inc=1, device_id=peer(here, offset), device_id_type=MESH)

    dims = (((0,), (0,)), ((), ()))
    for i in range(n):
        loads[i].wait()
        high, low = split(xb[i * CHUNK : (i + 1) * CHUNK, :])
        a = lax.dot_general(high, high, dims, preferred_element_type=F32)
        b = lax.dot_general(high, low, dims, preferred_element_type=F32)
        if i == 0:
            acc[...] = a
            cross[...] = b
        else:
            acc[...] += a
            cross[...] += b
    b = cross[...]
    total = acc[...] + b + b.T
    width = total.shape[1] // 2
    for half in range(2):
        part[half] = total[:, half * width : (half + 1) * width].reshape(64, 8, width)

    pl.semaphore_wait(barrier, 1 + len(OFFSETS))
    swap = pltpu.make_async_remote_copy(
        src_ref=part.at[1 - core],
        dst_ref=crecv,
        send_sem=core_sem.at[0],
        recv_sem=core_sem.at[1],
        device_id=twin,
        device_id_type=MESH,
    )
    swap.start()
    swap.wait()
    mine[...] = part[core] + crecv[...]

    def scatter(s, offset):
        dz, dx, dy = offset
        target = (((z + dz) % 4) * 4 + (x + dx) % 4) * 4 + (y + dy) % 4
        return pltpu.make_async_remote_copy(
            src_ref=mine.at[target],
            dst_ref=rbuf.at[s],
            send_sem=rs_sem.at[0],
            recv_sem=rs_sem.at[1],
            device_id=peer(here, offset),
            device_id_type=MESH,
        )

    for s, offset in enumerate(OFFSETS):
        scatter(s, offset).start()
    pltpu.make_async_copy(rbuf, rbuf, rs_sem.at[1]).wait()
    sums = [mine[chip]] + [rbuf[s] for s in range(63)]
    while len(sums) > 1:
        sums = [a + b for a, b in zip(sums[0::2], sums[1::2])]
    out[core, chip] = sums[0]
    for s, offset in enumerate(OFFSETS):
        pltpu.make_async_remote_copy(
            src_ref=out.at[core, chip],
            dst_ref=out.at[core, chip],
            send_sem=ag_sem.at[0],
            recv_sem=ag_sem.at[1],
            device_id=peer(here, offset),
            device_id_type=MESH,
        ).start()
    pltpu.make_async_copy(rbuf, rbuf, ag_sem.at[1]).wait()
    forward = pltpu.make_async_remote_copy(
        src_ref=out.at[core],
        dst_ref=out.at[core],
        send_sem=fw_sem.at[0],
        recv_sem=fw_sem.at[1],
        device_id=twin,
        device_id_type=MESH,
    )
    forward.start()
    pltpu.make_async_copy(rbuf, rbuf, rs_sem.at[0]).wait()
    pltpu.make_async_copy(rbuf, rbuf, ag_sem.at[0]).wait()
    forward.wait()


def sub_row(x, s):
    return jnp.broadcast_to(x[s : s + 1, :], (8, 128))


def lane_col(x, j):
    return jnp.broadcast_to(x[:, j : j + 1], (8, 128))


def invert_leaf(rows):
    lane = lax.broadcasted_iota(jnp.int32, (8, 128), 1)
    sub = lax.broadcasted_iota(jnp.int32, (8, 128), 0)
    rows = list(rows)
    pivots = jnp.ones((8, 128), F32)
    nv = GROUP // 8
    for g in range(128 // GROUP):
        a = GROUP * g
        own = [nv * g + v for v in range(nv)]
        others = [i for i in range(16) if i > own[-1]] + [i for i in range(16) if i < own[0]]
        cols = [[lane_col(rows[m], a + j) for m in own] for j in range(GROUP)]
        left = {i: [lane_col(rows[i], a + j) for j in range(GROUP)] for i in others}
        inside = (lane >= a) & (lane < a + GROUP)
        top = [jnp.where(inside, (lane - a == sub + 8 * v).astype(F32), rows[m]) for v, m in enumerate(own)]
        scale = [None] * nv
        for k in range(GROUP):
            kv, ks = divmod(k, 8)
            pivot = sub_row(cols[k][kv], ks)
            r = 1.0 / pivot
            pivots = jnp.where(lane == a + k, pivot, pivots)
            scale[kv] = r if scale[kv] is None else jnp.where(sub == ks, r, scale[kv])
            rest = [jnp.where(sub == ks, 0.0, cols[k][v]) if v == kv else cols[k][v] for v in range(nv)]
            factor = [rest[v] * r for v in range(nv)]
            for j in range(k + 1, GROUP):
                b = sub_row(cols[j][kv], ks)
                if j == k + 1:
                    cols[j] = [cols[j][v] - (rest[v] * b) * r for v in range(nv)]
                else:
                    cols[j] = [cols[j][v] - factor[v] * b for v in range(nv)]
            b = sub_row(top[kv], ks)
            top = [top[v] - factor[v] * b for v in range(nv)]
        top = [top[v] * scale[v] for v in range(nv)]
        for v, m in enumerate(own):
            rows[m] = top[v]
        spread = [sub_row(top[j // 8], j % 8) for j in range(GROUP)]
        for i in others:
            value = jnp.where(inside, 0.0, rows[i])
            for j in range(GROUP):
                value = value - left[i][j] * spread[j]
            rows[i] = value
    return rows, pivots


def dot_exact(a, b):
    return jnp.dot(a, b, precision=lax.Precision.HIGHEST, preferred_element_type=F32)


def map_kernel(total, gram, x_hbm, out_hbm, logdet, xb, ob, mat, load_sem, store_sem):
    rows, k = x_hbm.shape
    n = rows // CHUNK
    loads = [
        pltpu.make_async_copy(x_hbm.at[pl.ds(i * CHUNK, CHUNK)], xb.at[pl.ds(i * CHUNK, CHUNK)], load_sem.at[i])
        for i in range(n)
    ]
    for load in loads:
        load.start()
    half = k // 2
    eye = (lax.broadcasted_iota(jnp.int32, (k, k), 0) == lax.broadcasted_iota(jnp.int32, (k, k), 1)).astype(F32)
    mat[...] = eye
    for c in range(2):
        mat[:, c * half : (c + 1) * half] += gram[c].reshape(k, half) * (1.0 / total)

    logs = jnp.zeros((8, 128), F32)
    unit = eye[:128, :128]
    for b in range(k // 128):
        lo, hi = 128 * b, 128 * (b + 1)
        leaf, pivots = invert_leaf([mat[lo + 8 * i : lo + 8 * i + 8, lo:hi] for i in range(16)])
        logs = logs + jnp.log(pivots)
        inverse = jnp.concatenate(leaf, axis=0)
        mat[lo:hi, lo:hi] = unit
        top = dot_exact(inverse, mat[lo:hi, :])
        for i in range(k // 128):
            if i != b:
                side = mat[128 * i : 128 * i + 128, lo:hi]
                mat[128 * i : 128 * i + 128, lo:hi] = jnp.zeros((128, 128), F32)
                mat[128 * i : 128 * i + 128, :] -= dot_exact(side, top)
        mat[lo:hi, :] = top
    logdet[...] = jnp.broadcast_to(jnp.sum(logs[0:1, :], axis=1, keepdims=True), (8, 128)) * (1.0 / k)

    high, low = split(mat[...])
    stores = []
    for i in range(n):
        loads[i].wait()
        xh, xl = split(xb[i * CHUNK : (i + 1) * CHUNK, :])
        y = jnp.dot(xl, high, preferred_element_type=F32) + jnp.dot(xh, low, preferred_element_type=F32)
        ob[i * CHUNK : (i + 1) * CHUNK, :] = jnp.dot(xh, high, preferred_element_type=F32) + y
        store = pltpu.make_async_copy(
            ob.at[pl.ds(i * CHUNK, CHUNK)], out_hbm.at[pl.ds(i * CHUNK, CHUNK)], store_sem.at[i]
        )
        store.start()
        stores.append(store)
    for store in stores:
        store.wait()


def on_device(sketch):
    rows, k = sketch.shape
    total = rows * lax.axis_size("crow") * lax.axis_size("ccol")
    n = rows // CHUNK
    half = k // 2
    vmem, anywhere = pl.BlockSpec(memory_space=pltpu.VMEM), pl.BlockSpec(memory_space=pl.ANY)
    dma = pltpu.SemaphoreType.DMA
    gram = pl.pallas_call(
        gram_kernel,
        out_shape=jax.ShapeDtypeStruct((2, 64, 8, half), F32),
        in_specs=[anywhere],
        out_specs=vmem,
        scratch_shapes=[
            pltpu.VMEM((rows, k), F32),
            pltpu.VMEM((k, k), F32),
            pltpu.VMEM((k, k), F32),
            pltpu.VMEM((2, 64, 8, half), F32),
            pltpu.VMEM((64, 8, half), F32),
            pltpu.VMEM((64, 8, half), F32),
            pltpu.VMEM((63, 8, half), F32),
            dma((n,)),
            dma((2,)),
            dma((2,)),
            dma((2,)),
            dma((2,)),
        ],
        compiler_params=pltpu.CompilerParams(
            collective_id=0, has_side_effects=True, vmem_limit_bytes=VMEM_LIMIT
        ),
        name="gram_sum",
    )(sketch)
    basis, logdet = pl.pallas_call(
        functools.partial(map_kernel, total),
        out_shape=(jax.ShapeDtypeStruct((rows, k), F32), jax.ShapeDtypeStruct((8, 128), F32)),
        in_specs=[vmem, anywhere],
        out_specs=(anywhere, vmem),
        scratch_shapes=[
            pltpu.VMEM((rows, k), F32),
            pltpu.VMEM((rows, k), F32),
            pltpu.VMEM((k, k), F32),
            dma((n,)),
            dma((n,)),
        ],
        compiler_params=pltpu.CompilerParams(vmem_limit_bytes=VMEM_LIMIT),
        name="invert_and_map",
    )(gram, sketch)
    return basis, logdet[0, 0]


def solution(mesh):
    return jax.shard_map(
        on_device,
        mesh=mesh,
        in_specs=(P(("crow", "ccol"), None),),
        out_specs=(P(("crow", "ccol"), None), P()),
        check_vma=False,
    )
```

```python
import functools

import jax
import jax.numpy as jnp
from jax import lax
from jax.experimental import pallas as pl
from jax.experimental.pallas import tpu as pltpu
from jax.sharding import PartitionSpec as P

MESH = pl.DeviceIdType.MESH
F32, BF16 = jnp.float32, jnp.bfloat16
VMEM_LIMIT = 36 * 2**20
CHUNK = 512
GROUP = 16


def split(x):
    high = x.astype(BF16)
    return high, (x - high.astype(F32)).astype(BF16)


def place():
    crow, ccol = lax.axis_index("crow"), lax.axis_index("ccol")
    return crow // 4, crow % 4, ccol // 2, ccol % 2


def peer(here, offset):
    z, x, y, core = here
    dz, dx, dy = offset
    return (((z + dz) % 4) * 4 + (x + dx) % 4, ((y + dy) % 4) * 2 + core)


def hops(offset):
    return sum(min(d, 4 - d) for d in offset)


OFFSETS = sorted(
    [(dz, dx, dy) for dz in range(4) for dx in range(4) for dy in range(4) if (dz, dx, dy) != (0, 0, 0)],
    key=lambda o: (-hops(o), o),
)


def block_tiles(i, j):
    start = 8 * (i * (i + 1) // 2 + j)
    return slice(start, start + 8)


def first_tile(z, x, s):
    return 5 * (4 * z + x) + s + (s + 2) // 3


def gram_kernel(
    x_hbm, out, high, low, xb, acc, cross, part, crecv, mine, recv,
    load_sem, core_sem, rs_sem, rs2_sem, ag_sem, fw_sem,
):
    rows = x_hbm.shape[0]
    rbuf, rbuf2 = recv.at[pl.ds(0, 63)], recv.at[pl.ds(63, 64)]
    n = rows // CHUNK
    loads = [
        pltpu.make_async_copy(x_hbm.at[pl.ds(i * CHUNK, CHUNK)], xb.at[pl.ds(i * CHUNK, CHUNK)], load_sem.at[i])
        for i in range(n)
    ]
    for load in loads:
        load.start()

    here = place()
    z, x, y, core = here
    s = (x + y + z) % 4
    crow, ccol = lax.axis_index("crow"), lax.axis_index("ccol")
    twin = (crow, ccol + 1 - 2 * core)
    barrier = pltpu.get_barrier_semaphore()
    pl.semaphore_signal(barrier, inc=1, device_id=twin, device_id_type=MESH)
    for offset in OFFSETS:
        pl.semaphore_signal(barrier, inc=1, device_id=peer(here, offset), device_id_type=MESH)

    dims = (((0,), (0,)), ((), ()))
    for i in range(n):
        loads[i].wait()
        span = slice(i * CHUNK, (i + 1) * CHUNK)
        h, l = split(xb[span, :])
        high[span, :] = h
        low[span, :] = l
        a = lax.dot_general(h, h, dims, preferred_element_type=F32)
        b = lax.dot_general(h, l, dims, preferred_element_type=F32)
        if i == 0:
            acc[...] = a
            cross[...] = b
        else:
            acc[...] += a
            cross[...] += b
    for i in range(4):
        for j in range(i + 1):
            si, sj = slice(128 * i, 128 * i + 128), slice(128 * j, 128 * j + 128)
            block = (acc[si, sj] + (cross[si, sj] + cross[sj, si].T)).reshape(8, 2, 8, 128)
            for c in range(2):
                part[c, block_tiles(i, j)] = block[:, c]

    pl.semaphore_wait(barrier, 1 + len(OFFSETS))
    swap = pltpu.make_async_remote_copy(
        src_ref=part.at[1 - core],
        dst_ref=crecv,
        send_sem=core_sem.at[0],
        recv_sem=core_sem.at[1],
        device_id=twin,
        device_id_type=MESH,
    )
    swap.start()
    swap.wait()
    mine[...] = part[core] + crecv[...]

    for slot, offset in enumerate(OFFSETS):
        dz, dx, dy = offset
        tile = first_tile((z + dz) % 4, (x + dx) % 4, (s + dz + dx + dy) % 4)
        pltpu.make_async_remote_copy(
            src_ref=mine.at[tile],
            dst_ref=rbuf.at[slot],
            send_sem=rs_sem.at[0],
            recv_sem=rs_sem.at[1],
            device_id=peer(here, offset),
            device_id_type=MESH,
        ).start()

    def second(dz, dx):
        dy = (12 - s - dz - dx) % 4
        return pltpu.make_async_remote_copy(
            src_ref=mine.at[5 * (((z + dz) % 4) * 4 + (x + dx) % 4) + 1],
            dst_ref=rbuf2.at[16 * dz + 4 * dx + dy],
            send_sem=rs2_sem.at[0],
            recv_sem=rs2_sem.at[1],
            device_id=peer(here, (dz, dx, dy)),
            device_id_type=MESH,
        )

    for dz in (2, 1, 3, 0):
        for dx in (2, 1, 3, 0):
            if (dz, dx) != (0, 0):
                second(dz, dx).start()

    @pl.when(s != 0)
    def _():
        second(0, 0).start()

    def summed(values):
        while len(values) > 1:
            values = [a + b for a, b in zip(values[0::2], values[1::2])]
        return values[0]

    tile = first_tile(z, x, s)
    pltpu.make_async_copy(rbuf, rbuf, rs_sem.at[1]).wait()
    out[core, tile] = summed([mine[tile]] + [rbuf[slot] for slot in range(63)])

    def gather(count):
        for offset in OFFSETS:
            pltpu.make_async_remote_copy(
                src_ref=out.at[core, pl.ds(tile, count)],
                dst_ref=out.at[core, pl.ds(tile, count)],
                send_sem=ag_sem.at[0],
                recv_sem=ag_sem.at[1],
                device_id=peer(here, offset),
                device_id_type=MESH,
            ).start()
        rest = out.at[core, pl.ds(0, 80 - count)]
        pltpu.make_async_copy(rest, rest, ag_sem.at[1]).wait()

    @pl.when(s == 0)
    def _():
        others = rbuf2.at[pl.ds(1, 63)]
        pltpu.make_async_copy(others, others, rs2_sem.at[1]).wait()
        out[core, tile + 1] = summed([mine[tile + 1]] + [rbuf2[slot] for slot in range(1, 64)])
        gather(2)

    @pl.when(s != 0)
    def _():
        gather(1)

    forward = pltpu.make_async_remote_copy(
        src_ref=out.at[core],
        dst_ref=out.at[core],
        send_sem=fw_sem.at[0],
        recv_sem=fw_sem.at[1],
        device_id=twin,
        device_id_type=MESH,
    )
    forward.start()
    pltpu.make_async_copy(rbuf, rbuf, rs_sem.at[0]).wait()

    @pl.when(s == 0)
    def _():
        sent, both = rbuf2.at[pl.ds(0, 15)], recv.at[pl.ds(0, 126)]
        pltpu.make_async_copy(sent, sent, rs2_sem.at[0]).wait()
        pltpu.make_async_copy(both, both, ag_sem.at[0]).wait()

    @pl.when(s != 0)
    def _():
        sent = rbuf2.at[pl.ds(0, 16)]
        pltpu.make_async_copy(sent, sent, rs2_sem.at[0]).wait()
        pltpu.make_async_copy(rbuf, rbuf, ag_sem.at[0]).wait()

    forward.wait()


def sub_row(x, s):
    return jnp.broadcast_to(x[s : s + 1, :], (8, 128))


def lane_col(x, j):
    return jnp.broadcast_to(x[:, j : j + 1], (8, 128))


def invert_leaf(rows):
    lane = lax.broadcasted_iota(jnp.int32, (8, 128), 1)
    sub = lax.broadcasted_iota(jnp.int32, (8, 128), 0)
    rows = list(rows)
    dets = jnp.ones((8, 128), F32)
    zero = jnp.zeros((8, 128), F32)
    nv = GROUP // 8
    for g in range(128 // GROUP):
        a = GROUP * g
        own = [nv * g + v for v in range(nv)]
        near = [i for i in range(own[-1] + 1, own[-1] + 1 + nv) if i < 16]
        cols = [[lane_col(rows[m], a + j) for m in own] for j in range(GROUP)]
        left = {i: [lane_col(rows[i], a + j) for j in range(GROUP)] for i in near}
        inside = (lane >= a) & (lane < a + GROUP)
        top = [jnp.where(inside, (lane - a == sub + 8 * v).astype(F32), rows[m]) for v, m in enumerate(own)]
        diag, off = [zero] * nv, [zero] * nv
        for k in range(0, GROUP, 2):
            v0, s0 = divmod(k, 8)
            c0, c1 = cols[k], cols[k + 1]
            p00, p10 = sub_row(c0[v0], s0), sub_row(c0[v0], s0 + 1)
            p01, p11 = sub_row(c1[v0], s0), sub_row(c1[v0], s0 + 1)
            det = p00 * p11 - p01 * p10
            r = 1.0 / det
            dets = jnp.where(lane == a + k, det, dets)
            diag[v0] = jnp.where(sub == s0, p11 * r, jnp.where(sub == s0 + 1, p00 * r, diag[v0]))
            off[v0] = jnp.where(sub == s0, -p01 * r, jnp.where(sub == s0 + 1, -p10 * r, off[v0]))
            n0 = [c0[v] * p11 - c1[v] * p10 for v in range(nv)]
            n1 = [c1[v] * p00 - c0[v] * p01 for v in range(nv)]
            pair = (sub == s0) | (sub == s0 + 1)
            n0[v0] = jnp.where(pair, 0.0, n0[v0])
            n1[v0] = jnp.where(pair, 0.0, n1[v0])
            f0, f1 = [n * r for n in n0], [n * r for n in n1]
            for j in range(k + 2, GROUP):
                b0, b1 = sub_row(cols[j][v0], s0), sub_row(cols[j][v0], s0 + 1)
                if j < k + 4:
                    cols[j] = [cols[j][v] - (n0[v] * b0 + n1[v] * b1) * r for v in range(nv)]
                else:
                    cols[j] = [cols[j][v] - (f0[v] * b0 + f1[v] * b1) for v in range(nv)]
            b0, b1 = sub_row(top[v0], s0), sub_row(top[v0], s0 + 1)
            top = [top[v] - (f0[v] * b0 + f1[v] * b1) for v in range(nv)]
        swapped = [jnp.where(sub % 2 == 0, pltpu.roll(t, 7, 0), pltpu.roll(t, 1, 0)) for t in top]
        top = [diag[v] * top[v] + off[v] * swapped[v] for v in range(nv)]
        spread = [sub_row(top[j // 8], j % 8) for j in range(GROUP)]
        new = dict(zip(own, top))
        for i in near:
            terms = [left[i][j] * spread[j] for j in range(GROUP)]
            while len(terms) > 1:
                terms = [s + t for s, t in zip(terms[0::2], terms[1::2])]
            new[i] = jnp.where(inside, 0.0, rows[i]) - terms[0]
        padded = [jnp.zeros((a, 128), F32)] * (a > 0) + top + [jnp.zeros((128 - a - GROUP, 128), F32)] * (a + GROUP < 128)
        padded = jnp.concatenate(padded, axis=0)
        for start, stop in ((0, own[0]), (own[-1] + 1 + len(near), 16)):
            if stop > start:
                update = dot_exact(jnp.concatenate(rows[start:stop], axis=0), padded)
                for i in range(start, stop):
                    new[i] = jnp.where(inside, 0.0, rows[i]) - update[8 * (i - start) : 8 * (i - start) + 8]
        rows = [new[i] for i in range(16)]
    return rows, dets


def dot_exact(a, b):
    return jnp.dot(a, b, precision=lax.Precision.HIGHEST, preferred_element_type=F32)


def map_kernel(total, gram, high, low, out_hbm, logdet, ob, mat, store_sem):
    rows, k = high.shape
    n = rows // CHUNK
    eye = lax.broadcasted_iota(jnp.int32, (128, 128), 0) == lax.broadcasted_iota(jnp.int32, (128, 128), 1)
    for i in range(k // 128):
        for j in range(i + 1):
            tiles = block_tiles(i, j)
            block = jnp.stack([gram[0, tiles], gram[1, tiles]], axis=1).reshape(128, 128) * (1.0 / total)
            if i == j:
                block = block + eye.astype(F32)
            else:
                mat[128 * j : 128 * j + 128, 128 * i : 128 * i + 128] = block.T
            mat[128 * i : 128 * i + 128, 128 * j : 128 * j + 128] = block

    logs = jnp.zeros((8, 128), F32)
    count = k // 128
    block = mat[:128, :128]
    for b in range(count):
        lo, hi = 128 * b, 128 * (b + 1)
        leaf, dets = invert_leaf([block[8 * i : 8 * i + 8] for i in range(16)])
        logs = logs + jnp.log(dets)
        inverse = jnp.concatenate(leaf, axis=0)
        sides = [mat[128 * i : 128 * i + 128, lo:hi] for i in range(count)]
        if b + 1 < count:
            first = dot_exact(inverse, mat[lo:hi, hi : hi + 128])
            block = mat[hi : hi + 128, hi : hi + 128] - dot_exact(sides[b + 1], first)
        parts = []
        if lo:
            parts.append(dot_exact(inverse, mat[lo:hi, :lo]))
        parts.append(inverse)
        if b + 1 < count:
            parts.append(first)
        if hi + 128 < k:
            parts.append(dot_exact(inverse, mat[lo:hi, hi + 128 :]))
        top = jnp.concatenate(parts, axis=1)
        for i in range(count):
            if i != b:
                update = dot_exact(sides[i], top)
                for j in range(count):
                    rows_i, cols_j = slice(128 * i, 128 * i + 128), slice(128 * j, 128 * j + 128)
                    if j == b:
                        mat[rows_i, cols_j] = -update[:, cols_j]
                    else:
                        mat[rows_i, cols_j] -= update[:, cols_j]
        mat[lo:hi, :] = top
    logdet[0, 0] = jnp.sum(logs[0:1, :]) * (1.0 / k)

    mh, ml = split(mat[...])
    stores = []
    for i in range(n):
        span = slice(i * CHUNK, (i + 1) * CHUNK)
        xh = high[span, :]
        y = jnp.dot(low[span, :], mh, preferred_element_type=F32) + jnp.dot(xh, ml, preferred_element_type=F32)
        ob[span, :] = jnp.dot(xh, mh, preferred_element_type=F32) + y
        store = pltpu.make_async_copy(
            ob.at[pl.ds(i * CHUNK, CHUNK)], out_hbm.at[pl.ds(i * CHUNK, CHUNK)], store_sem.at[i]
        )
        store.start()
        stores.append(store)
    for store in stores:
        store.wait()


VMEM, HBM = pl.BlockSpec(memory_space=pltpu.VMEM), pl.BlockSpec(memory_space=pltpu.HBM)
DMA = pltpu.SemaphoreType.DMA


def gram_sum(sketch):
    rows, k = sketch.shape
    return pl.pallas_call(
        gram_kernel,
        out_shape=(
            jax.ShapeDtypeStruct((2, 80, 8, 128), F32),
            jax.ShapeDtypeStruct((rows, k), BF16),
            jax.ShapeDtypeStruct((rows, k), BF16),
        ),
        in_specs=[HBM],
        out_specs=(VMEM, VMEM, VMEM),
        scratch_shapes=[
            pltpu.VMEM((rows, k), F32),
            pltpu.VMEM((k, k), F32),
            pltpu.VMEM((k, k), F32),
            pltpu.VMEM((2, 80, 8, 128), F32),
            pltpu.VMEM((80, 8, 128), F32),
            pltpu.VMEM((80, 8, 128), F32),
            pltpu.VMEM((127, 8, 128), F32),
            DMA((rows // CHUNK,)),
            DMA((2,)),
            DMA((2,)),
            DMA((2,)),
            DMA((2,)),
            DMA((2,)),
        ],
        compiler_params=pltpu.CompilerParams(
            collective_id=0, has_side_effects=True, vmem_limit_bytes=VMEM_LIMIT
        ),
        name="gram_sum",
    )(sketch)


def invert_and_map(gram, high, low, total):
    rows, k = high.shape
    return pl.pallas_call(
        functools.partial(map_kernel, total),
        out_shape=(jax.ShapeDtypeStruct((rows, k), F32), jax.ShapeDtypeStruct((1, 1), F32)),
        in_specs=[VMEM, VMEM, VMEM],
        out_specs=(HBM, pl.BlockSpec(memory_space=pltpu.SMEM)),
        scratch_shapes=[
            pltpu.VMEM((rows, k), F32),
            pltpu.VMEM((k, k), F32),
            DMA((rows // CHUNK,)),
        ],
        compiler_params=pltpu.CompilerParams(vmem_limit_bytes=VMEM_LIMIT),
        name="invert_and_map",
    )(gram, high, low)


def on_device(sketch):
    total = sketch.shape[0] * lax.axis_size("crow") * lax.axis_size("ccol")
    basis, logdet = invert_and_map(*gram_sum(pltpu.with_memory_space_constraint(sketch, pltpu.HBM)), total)
    return basis, logdet.reshape(())


def solution(mesh):
    return jax.shard_map(
        on_device,
        mesh=mesh,
        in_specs=(P(("crow", "ccol"), None),),
        out_specs=(P(("crow", "ccol"), None), P()),
        check_vma=False,
    )
```

```python
import functools

import jax
import jax.numpy as jnp
from jax import lax
from jax.experimental import pallas as pl
from jax.experimental.pallas import tpu as pltpu
from jax.sharding import PartitionSpec as P

MESH = pl.DeviceIdType.MESH
F32, BF16 = jnp.float32, jnp.bfloat16
VMEM_LIMIT = 36 * 2**20
CHUNK = 512
STORE = 256
GROUP = 16
FORWARD_AFTER = 5


def split(x):
    high = x.astype(BF16)
    return high, (x - high.astype(F32)).astype(BF16)


def place():
    crow, ccol = lax.axis_index("crow"), lax.axis_index("ccol")
    return crow // 4, crow % 4, ccol // 2, ccol % 2


def peer(here, offset):
    z, x, y, core = here
    dz, dx, dy = offset
    return (((z + dz) % 4) * 4 + (x + dx) % 4, ((y + dy) % 4) * 2 + core)


def hops(offset):
    return sum(min(d, 4 - d) for d in offset)


OFFSETS = sorted(
    [(dz, dx, dy) for dz in range(4) for dx in range(4) for dy in range(4) if (dz, dx, dy) != (0, 0, 0)],
    key=lambda o: (-hops(o), o),
)


def block_tiles(i, j):
    start = 8 * (i * (i + 1) // 2 + j)
    return slice(start, start + 8)


def load_block(tiles_ref, i, j, total):
    tiles = block_tiles(i, j)
    return jnp.stack([tiles_ref[0, tiles], tiles_ref[1, tiles]], axis=1).reshape(128, 128) * (1.0 / total)


def unit(n):
    return (lax.broadcasted_iota(jnp.int32, (n, n), 0) == lax.broadcasted_iota(jnp.int32, (n, n), 1)).astype(F32)


def gram_kernel(
    total, x_hbm, out, high, low, inverse, first, dets, xb, acc, cross, part, crecv, mine, recv,
    load_sem, core_sem, rs_sem, rs2_sem, ag_sem, ag2_sem, fw_sem, fw2_sem,
):
    rows = x_hbm.shape[0]
    rbuf, rbuf2 = recv.at[pl.ds(0, 63)], recv.at[pl.ds(63, 64)]
    n = rows // CHUNK
    loads = [
        pltpu.make_async_copy(x_hbm.at[pl.ds(i * CHUNK, CHUNK)], xb.at[pl.ds(i * CHUNK, CHUNK)], load_sem.at[i])
        for i in range(n)
    ]
    for load in loads:
        load.start()

    here = place()
    z, x, y, core = here
    s = (x + y + z) % 4
    crow, ccol = lax.axis_index("crow"), lax.axis_index("ccol")
    twin = (crow, ccol + 1 - 2 * core)
    barrier = pltpu.get_barrier_semaphore()
    pl.semaphore_signal(barrier, inc=1, device_id=twin, device_id_type=MESH)
    for offset in OFFSETS:
        pl.semaphore_signal(barrier, inc=1, device_id=peer(here, offset), device_id_type=MESH)

    dims = (((0,), (0,)), ((), ()))
    for i in range(n):
        loads[i].wait()
        span = slice(i * CHUNK, (i + 1) * CHUNK)
        h, l = split(xb[span, :])
        high[span, :] = h
        low[span, :] = l
        a = lax.dot_general(h, h, dims, preferred_element_type=F32)
        b = lax.dot_general(h, l, dims, preferred_element_type=F32)
        if i == 0:
            acc[...] = a
            cross[...] = b
        else:
            acc[...] += a
            cross[...] += b
    for i in range(4):
        for j in range(i + 1):
            si, sj = slice(128 * i, 128 * i + 128), slice(128 * j, 128 * j + 128)
            block = (acc[si, sj] + (cross[si, sj] + cross[sj, si].T)).reshape(8, 2, 8, 128)
            for c in range(2):
                part[c, block_tiles(i, j)] = block[:, c]

    pl.semaphore_wait(barrier, 1 + len(OFFSETS))
    swap = pltpu.make_async_remote_copy(
        src_ref=part.at[1 - core],
        dst_ref=crecv,
        send_sem=core_sem.at[0],
        recv_sem=core_sem.at[1],
        device_id=twin,
        device_id_type=MESH,
    )
    swap.start()
    swap.wait()
    mine[...] = part[core] + crecv[...]

    def second(dz, dx):
        dy = (12 - s - dz - dx) % 4
        return pltpu.make_async_remote_copy(
            src_ref=mine.at[((z + dz) % 4) * 4 + (x + dx) % 4],
            dst_ref=rbuf2.at[16 * dz + 4 * dx + dy],
            send_sem=rs2_sem.at[0],
            recv_sem=rs2_sem.at[1],
            device_id=peer(here, (dz, dx, dy)),
            device_id_type=MESH,
        )

    for dz in (2, 1, 3, 0):
        for dx in (2, 1, 3, 0):
            if (dz, dx) != (0, 0):
                second(dz, dx).start()

    @pl.when(s != 0)
    def _():
        second(0, 0).start()

    for slot, offset in enumerate(OFFSETS):
        dz, dx, dy = offset
        pltpu.make_async_remote_copy(
            src_ref=mine.at[16 + (((z + dz) % 4) * 4 + (x + dx) % 4) * 4 + (y + dy) % 4],
            dst_ref=rbuf.at[slot],
            send_sem=rs_sem.at[0],
            recv_sem=rs_sem.at[1],
            device_id=peer(here, offset),
            device_id_type=MESH,
        ).start()

    def summed(values):
        while len(values) > 1:
            values = [a + b for a, b in zip(values[0::2], values[1::2])]
        return values[0]

    def gather(tile, sem):
        for offset in OFFSETS:
            pltpu.make_async_remote_copy(
                src_ref=out.at[core, tile],
                dst_ref=out.at[core, tile],
                send_sem=sem.at[0],
                recv_sem=sem.at[1],
                device_id=peer(here, offset),
                device_id_type=MESH,
            ).start()

    def forward(tiles, sem):
        return pltpu.make_async_remote_copy(
            src_ref=out.at[core, tiles],
            dst_ref=out.at[core, tiles],
            send_sem=sem.at[0],
            recv_sem=sem.at[1],
            device_id=twin,
            device_id_type=MESH,
        )

    def settle(ref, sem):
        pltpu.make_async_copy(ref, ref, sem).wait()

    @pl.when(s == 0)
    def _():
        settle(rbuf2.at[pl.ds(1, 63)], rs2_sem.at[1])
        out[core, 4 * z + x] = summed([mine[4 * z + x]] + [rbuf2[slot] for slot in range(1, 64)])
        gather(4 * z + x, ag2_sem)

    chip = (z * 4 + x) * 4 + y
    settle(rbuf, rs_sem.at[1])
    out[core, 16 + chip] = summed([mine[16 + chip]] + [rbuf[slot] for slot in range(63)])
    gather(16 + chip, ag_sem)

    @pl.when(s == 0)
    def _():
        settle(rbuf2.at[pl.ds(0, 15)], ag2_sem.at[1])

    @pl.when(s != 0)
    def _():
        settle(rbuf2.at[pl.ds(0, 16)], ag2_sem.at[1])

    ahead = forward(pl.ds(0, 16), fw2_sem)
    ahead.start()
    ahead.wait_recv()
    later = forward(pl.ds(16, 64), fw_sem)
    calls = iter(range(8))

    def between():
        if next(calls) == FORWARD_AFTER:
            settle(rbuf, ag_sem.at[1])
            later.start()

    block = load_block(out, 0, 0, total) + unit(128)
    leaf, dets[...] = invert_leaf([block[8 * i : 8 * i + 8] for i in range(16)], between)
    leaf = jnp.concatenate(leaf, axis=0)
    inverse[...] = leaf
    first[...] = dot_exact(leaf, load_block(out, 1, 0, total).T)

    settle(rbuf, rs_sem.at[0])
    settle(rbuf, ag_sem.at[0])

    @pl.when(s == 0)
    def _():
        settle(rbuf2.at[pl.ds(0, 15)], rs2_sem.at[0])
        settle(rbuf, ag2_sem.at[0])

    @pl.when(s != 0)
    def _():
        settle(rbuf2.at[pl.ds(0, 16)], rs2_sem.at[0])

    ahead.wait_send()
    later.wait()


def sub_row(x, s):
    return jnp.broadcast_to(x[s : s + 1, :], (8, 128))


def lane_col(x, j):
    return jnp.broadcast_to(x[:, j : j + 1], (8, 128))


def invert_leaf(rows, between):
    lane = lax.broadcasted_iota(jnp.int32, (8, 128), 1)
    sub = lax.broadcasted_iota(jnp.int32, (8, 128), 0)
    rows = list(rows)
    dets = jnp.ones((8, 128), F32)
    zero = jnp.zeros((8, 128), F32)
    nv = GROUP // 8
    for g in range(128 // GROUP):
        a = GROUP * g
        own = [nv * g + v for v in range(nv)]
        near = [i for i in range(own[-1] + 1, own[-1] + 1 + nv) if i < 16]
        cols = [[lane_col(rows[m], a + j) for m in own] for j in range(GROUP)]
        left = {i: [lane_col(rows[i], a + j) for j in range(GROUP)] for i in near}
        inside = (lane >= a) & (lane < a + GROUP)
        top = [jnp.where(inside, (lane - a == sub + 8 * v).astype(F32), rows[m]) for v, m in enumerate(own)]
        diag, off = [zero] * nv, [zero] * nv
        for k in range(0, GROUP, 2):
            v0, s0 = divmod(k, 8)
            c0, c1 = cols[k], cols[k + 1]
            p00, p10 = sub_row(c0[v0], s0), sub_row(c0[v0], s0 + 1)
            p01, p11 = sub_row(c1[v0], s0), sub_row(c1[v0], s0 + 1)
            det = p00 * p11 - p01 * p10
            r = 1.0 / det
            dets = jnp.where(lane == a + k, det, dets)
            diag[v0] = jnp.where(sub == s0, p11 * r, jnp.where(sub == s0 + 1, p00 * r, diag[v0]))
            off[v0] = jnp.where(sub == s0, -p01 * r, jnp.where(sub == s0 + 1, -p10 * r, off[v0]))
            n0 = [c0[v] * p11 - c1[v] * p10 for v in range(nv)]
            n1 = [c1[v] * p00 - c0[v] * p01 for v in range(nv)]
            pair = (sub == s0) | (sub == s0 + 1)
            n0[v0] = jnp.where(pair, 0.0, n0[v0])
            n1[v0] = jnp.where(pair, 0.0, n1[v0])
            f0, f1 = [n * r for n in n0], [n * r for n in n1]
            for j in range(k + 2, GROUP):
                b0, b1 = sub_row(cols[j][v0], s0), sub_row(cols[j][v0], s0 + 1)
                if j < k + 4:
                    cols[j] = [cols[j][v] - (n0[v] * b0 + n1[v] * b1) * r for v in range(nv)]
                else:
                    cols[j] = [cols[j][v] - (f0[v] * b0 + f1[v] * b1) for v in range(nv)]
            b0, b1 = sub_row(top[v0], s0), sub_row(top[v0], s0 + 1)
            top = [top[v] - (f0[v] * b0 + f1[v] * b1) for v in range(nv)]
        swapped = [jnp.where(sub % 2 == 0, pltpu.roll(t, 7, 0), pltpu.roll(t, 1, 0)) for t in top]
        top = [diag[v] * top[v] + off[v] * swapped[v] for v in range(nv)]
        spread = [sub_row(top[j // 8], j % 8) for j in range(GROUP)]
        new = dict(zip(own, top))
        for i in near:
            terms = [left[i][j] * spread[j] for j in range(GROUP)]
            while len(terms) > 1:
                terms = [s + t for s, t in zip(terms[0::2], terms[1::2])]
            new[i] = jnp.where(inside, 0.0, rows[i]) - terms[0]
        padded = [jnp.zeros((a, 128), F32)] * (a > 0) + top + [jnp.zeros((128 - a - GROUP, 128), F32)] * (a + GROUP < 128)
        padded = jnp.concatenate(padded, axis=0)
        for start, stop in ((0, own[0]), (own[-1] + 1 + len(near), 16)):
            if stop > start:
                update = dot_exact(jnp.concatenate(rows[start:stop], axis=0), padded)
                for i in range(start, stop):
                    new[i] = jnp.where(inside, 0.0, rows[i]) - update[8 * (i - start) : 8 * (i - start) + 8]
        rows = [new[i] for i in range(16)]
        between()
    return rows, dets


def dot_exact(a, b):
    return jnp.dot(a, b, precision=lax.Precision.HIGHEST, preferred_element_type=F32)


def dot3(a, b):
    (ah, al), (bh, bl) = a, b
    small = jnp.dot(al, bh, preferred_element_type=F32) + jnp.dot(ah, bl, preferred_element_type=F32)
    return jnp.dot(ah, bh, preferred_element_type=F32) + small


def map_kernel(total, gram, high, low, inverse0, first0, dets0, out_hbm, logdet, ob, zh, zl, mat, store_sem):
    rows, k = high.shape
    n = rows // CHUNK
    for i in range(k // 128):
        for j in range(i + 1):
            block = load_block(gram, i, j, total)
            if i == j:
                block = block + unit(128)
            else:
                mat[128 * j : 128 * j + 128, 128 * i : 128 * i + 128] = block.T
            mat[128 * i : 128 * i + 128, 128 * j : 128 * j + 128] = block

    half, count = k // 2, k // 128
    early = iter(range(n))
    weights = []

    def forward_chunk():
        i = next(early, None)
        if i is None:
            return
        if not weights:
            weights.extend(split(mat[:half, :]))
        span = slice(i * CHUNK, (i + 1) * CHUNK)
        d = dot3((high[span, :half], low[span, :half]), weights)
        ob[span, :half] = d[:, :half]
        zh[span, :], zl[span, :] = split((high[span, half:].astype(F32) + low[span, half:].astype(F32)) - d[:, half:])

    logs = jnp.log(dets0[...])
    for b in range(count):
        lo, hi = 128 * b, 128 * (b + 1)
        base = 0 if lo < half else half
        if b == 0:
            inverse = inverse0[...]
        else:
            leaf, dets = invert_leaf(
                [block[8 * i : 8 * i + 8] for i in range(16)], forward_chunk if base else lambda: None
            )
            logs = logs + jnp.log(dets)
            inverse = jnp.concatenate(leaf, axis=0)
        sides = {i: mat[128 * i : 128 * i + 128, lo:hi] for i in range(base // 128, count)}
        if b + 1 < count:
            first = dot_exact(inverse, mat[lo:hi, hi : hi + 128]) if b else first0[...]
            block = mat[hi : hi + 128, hi : hi + 128] - dot_exact(sides[b + 1], first)
        parts = []
        if lo > base:
            parts.append(dot_exact(inverse, mat[lo:hi, base:lo]))
        parts.append(inverse)
        if b + 1 < count:
            parts.append(first)
        if hi + 128 < k:
            parts.append(dot_exact(inverse, mat[lo:hi, hi + 128 :]))
        top = jnp.concatenate(parts, axis=1)
        for i in sides:
            if i != b:
                update = dot_exact(sides[i], top)
                for j in sides:
                    rows_i, cols_j = slice(128 * i, 128 * i + 128), slice(128 * j, 128 * j + 128)
                    change = update[:, 128 * j - base : 128 * j - base + 128]
                    if j == b:
                        mat[rows_i, cols_j] = -change
                    else:
                        mat[rows_i, cols_j] -= change
        mat[lo:hi, base:] = top
    logdet[0, 0] = jnp.sum(logs[0:1, :]) * (1.0 / k)

    tail = split(mat[half:, half:])
    back = split(dot_exact(mat[half:, half:], mat[half:, :half]))
    stores = []
    for i in range(rows // STORE):
        span = slice(i * STORE, (i + 1) * STORE)
        z = zh[span, :], zl[span, :]
        ob[span, half:] = dot3(z, tail)
        ob[span, :half] += dot3(z, back)
        store = pltpu.make_async_copy(
            ob.at[pl.ds(i * STORE, STORE)], out_hbm.at[pl.ds(i * STORE, STORE)], store_sem.at[i]
        )
        store.start()
        stores.append(store)
    for store in stores:
        store.wait()


VMEM, HBM = pl.BlockSpec(memory_space=pltpu.VMEM), pl.BlockSpec(memory_space=pltpu.HBM)
DMA = pltpu.SemaphoreType.DMA


def gram_sum(sketch, total):
    rows, k = sketch.shape
    return pl.pallas_call(
        functools.partial(gram_kernel, total),
        out_shape=(
            jax.ShapeDtypeStruct((2, 80, 8, 128), F32),
            jax.ShapeDtypeStruct((rows, k), BF16),
            jax.ShapeDtypeStruct((rows, k), BF16),
            jax.ShapeDtypeStruct((128, 128), F32),
            jax.ShapeDtypeStruct((128, 128), F32),
            jax.ShapeDtypeStruct((8, 128), F32),
        ),
        in_specs=[HBM],
        out_specs=(VMEM,) * 6,
        scratch_shapes=[
            pltpu.VMEM((rows, k), F32),
            pltpu.VMEM((k, k), F32),
            pltpu.VMEM((k, k), F32),
            pltpu.VMEM((2, 80, 8, 128), F32),
            pltpu.VMEM((80, 8, 128), F32),
            pltpu.VMEM((80, 8, 128), F32),
            pltpu.VMEM((127, 8, 128), F32),
            DMA((rows // CHUNK,)),
        ]
        + [DMA((2,))] * 7,
        compiler_params=pltpu.CompilerParams(
            collective_id=0, has_side_effects=True, vmem_limit_bytes=VMEM_LIMIT
        ),
        name="gram_sum",
    )(pltpu.with_memory_space_constraint(sketch, pltpu.HBM))


def invert_and_map(total, gram, high, low, inverse, first, dets):
    rows, k = high.shape
    return pl.pallas_call(
        functools.partial(map_kernel, total),
        out_shape=(jax.ShapeDtypeStruct((rows, k), F32), jax.ShapeDtypeStruct((1, 1), F32)),
        in_specs=[VMEM] * 6,
        out_specs=(HBM, pl.BlockSpec(memory_space=pltpu.SMEM)),
        scratch_shapes=[
            pltpu.VMEM((rows, k), F32),
            pltpu.VMEM((rows, k // 2), BF16),
            pltpu.VMEM((rows, k // 2), BF16),
            pltpu.VMEM((k, k), F32),
            DMA((rows // STORE,)),
        ],
        compiler_params=pltpu.CompilerParams(vmem_limit_bytes=VMEM_LIMIT),
        name="invert_and_map",
    )(gram, high, low, inverse, first, dets)


def on_device(sketch):
    total = sketch.shape[0] * lax.axis_size("crow") * lax.axis_size("ccol")
    basis, logdet = invert_and_map(total, *gram_sum(sketch, total))
    return basis, logdet.reshape(())


def solution(mesh):
    return jax.shard_map(
        on_device,
        mesh=mesh,
        in_specs=(P(("crow", "ccol"), None),),
        out_specs=(P(("crow", "ccol"), None), P()),
        check_vma=False,
    )
```

```python
import functools

import jax
import jax.numpy as jnp
from jax import lax
from jax.experimental import pallas as pl
from jax.experimental.pallas import tpu as pltpu
from jax.sharding import PartitionSpec as P

MESH = pl.DeviceIdType.MESH
F32, BF16 = jnp.float32, jnp.bfloat16
VMEM_LIMIT = 36 * 2**20
CHUNK = 512
STORE = 256
GROUP = 16
FORWARD_AFTER = 6


def split(x):
    high = x.astype(BF16)
    return high, (x - high.astype(F32)).astype(BF16)


def place():
    crow, ccol = lax.axis_index("crow"), lax.axis_index("ccol")
    return crow // 4, crow % 4, ccol // 2, ccol % 2


def peer(here, offset, other=False):
    z, x, y, core = here
    dz, dx, dy = offset
    return (((z + dz) % 4) * 4 + (x + dx) % 4, ((y + dy) % 4) * 2 + (1 - core if other else core))


def hops(offset):
    return sum(min(d, 4 - d) for d in offset)


OFFSETS = sorted(
    [(dz, dx, dy) for dz in range(4) for dx in range(4) for dy in range(4) if (dz, dx, dy) != (0, 0, 0)],
    key=lambda o: (-hops(o), o),
)


def opposite(offset):
    return tuple((d + 2) % 4 for d in offset)


NEAR = [o for o in OFFSETS if (hops(o), o) < (hops(opposite(o)), opposite(o))]
EARLY = 32


def early_tile(z, x, s):
    flip = 2 * (s // 2)
    return 4 * ((z + flip) % 4) + (x + flip) % 4 + 16 * (s % 2)


def block_tiles(i, j):
    start = 8 * (i * (i + 1) // 2 + j)
    return slice(start, start + 8)


def load_block(tiles_ref, i, j, total):
    tiles = block_tiles(i, j)
    return jnp.stack([tiles_ref[0, tiles], tiles_ref[1, tiles]], axis=1).reshape(128, 128) * (1.0 / total)


def unit(n):
    return (lax.broadcasted_iota(jnp.int32, (n, n), 0) == lax.broadcasted_iota(jnp.int32, (n, n), 1)).astype(F32)


def gram_kernel(
    total, x_hbm, out, high, low, inverse0, first0, inverse1, dets, xb, acc, cross, part, crecv, mine, recv,
    load_sem, swap_sem, swap2_sem, rs_sem, rs2_sem, ag_sem, ag2_sem, fw_sem,
):
    rows = x_hbm.shape[0]
    rbuf, rbuf2 = recv.at[pl.ds(0, 63)], recv.at[pl.ds(63, 64)]
    n = rows // CHUNK
    loads = [
        pltpu.make_async_copy(x_hbm.at[pl.ds(i * CHUNK, CHUNK)], xb.at[pl.ds(i * CHUNK, CHUNK)], load_sem.at[i])
        for i in range(n)
    ]
    for load in loads:
        load.start()

    here = place()
    z, x, y, core = here
    s = (x + y + z) % 4
    twin = peer(here, (0, 0, 0), True)
    barrier = pltpu.get_barrier_semaphore()
    greeted = [peer(here, offset) for offset in OFFSETS]
    greeted += [peer(here, tuple((4 - d) % 4 for d in offset), True) for offset in NEAR]
    greeted.append(twin)

    def greet(devices):
        for device in devices:
            pl.semaphore_signal(barrier, inc=1, device_id=device, device_id_type=MESH)

    greet(greeted[:48])
    dims = (((0,), (0,)), ((), ()))
    for i in range(n):
        loads[i].wait()
        span = slice(i * CHUNK, (i + 1) * CHUNK)
        h, l = split(xb[span, :])
        high[span, :] = h
        low[span, :] = l
        a0 = lax.dot_general(h[:, :256], h[:, :256], dims, preferred_element_type=F32)
        a1 = lax.dot_general(h[:, 256:], h, dims, preferred_element_type=F32)
        b = lax.dot_general(h, l, dims, preferred_element_type=F32)
        if i == 0:
            acc[:256, :256] = a0
            acc[256:, :] = a1
            cross[...] = b
            greet(greeted[48:])
        else:
            acc[:256, :256] += a0
            acc[256:, :] += a1
            cross[...] += b

    def fill(blocks):
        for i, j in blocks:
            si, sj = slice(128 * i, 128 * i + 128), slice(128 * j, 128 * j + 128)
            block = (acc[si, sj] + (cross[si, sj] + cross[sj, si].T)).reshape(8, 2, 8, 128)
            for c in range(2):
                part[c, block_tiles(i, j)] = block[:, c]

    def swap(tiles, sem):
        return pltpu.make_async_remote_copy(
            src_ref=part.at[1 - core, tiles],
            dst_ref=crecv.at[tiles],
            send_sem=sem.at[0],
            recv_sem=sem.at[1],
            device_id=twin,
            device_id_type=MESH,
        )

    fill([(0, 0), (1, 0), (1, 1), (2, 0)])
    pl.semaphore_wait(barrier, len(greeted))
    swap_early, swap_late = swap(pl.ds(0, EARLY), swap_sem), swap(pl.ds(EARLY, 80 - EARLY), swap2_sem)
    swap_early.start()
    fill([(2, 1), (2, 2), (3, 0), (3, 1), (3, 2), (3, 3)])
    swap_late.start()
    swap_early.wait_recv()
    mine[:EARLY] = part[core, :EARLY] + crecv[:EARLY]
    for slot, offset in enumerate(OFFSETS):
        dz, dx, dy = offset
        pltpu.make_async_remote_copy(
            src_ref=mine.at[early_tile((z + dz) % 4, (x + dx) % 4, (s + dz + dx + dy) % 4)],
            dst_ref=rbuf.at[slot],
            send_sem=rs_sem.at[0],
            recv_sem=rs_sem.at[1],
            device_id=peer(here, offset),
            device_id_type=MESH,
        ).start()
    swap_late.wait_recv()
    mine[EARLY:] = part[core, EARLY:] + crecv[EARLY:]

    def late_tile(dz, dx, t):
        return EARLY + 3 * (4 * ((z + dz) % 4) + (x + dx) % 4) + t - 1

    def scatter_late(dz, dx, t):
        dy = (t + 12 - s - dz - dx) % 4
        return pltpu.make_async_remote_copy(
            src_ref=mine.at[late_tile(dz, dx, t)],
            dst_ref=rbuf2.at[16 * dz + 4 * dx + dy],
            send_sem=rs2_sem.at[0],
            recv_sem=rs2_sem.at[1],
            device_id=peer(here, (dz, dx, dy)),
            device_id_type=MESH,
        )

    for dz in (2, 1, 3, 0):
        for dx in (2, 1, 3, 0):
            if (dz, dx) != (0, 0):
                for t in (1, 2, 3):
                    scatter_late(dz, dx, t).start()
    for t in (1, 2, 3):

        @pl.when(s != t)
        def _():
            scatter_late(0, 0, t).start()

    def summed(values):
        while len(values) > 1:
            values = [a + b for a, b in zip(values[0::2], values[1::2])]
        return values[0]

    def send_sum(tile, sem, device):
        pltpu.make_async_remote_copy(
            src_ref=out.at[core, tile],
            dst_ref=out.at[core, tile],
            send_sem=sem.at[0],
            recv_sem=sem.at[1],
            device_id=device,
            device_id_type=MESH,
        ).start()

    def settle(ref, sem):
        pltpu.make_async_copy(ref, ref, sem).wait()

    tile = early_tile(z, x, s)
    settle(rbuf, rs_sem.at[1])
    terms = {offset: rbuf[slot] for slot, offset in enumerate(OFFSETS)}
    terms[0, 0, 0] = mine[tile]
    out[core, tile] = summed([terms[o] + terms[opposite(o)] for o in [(0, 0, 0)] + NEAR])
    for offset in NEAR:
        for other in (False, True):
            send_sum(tile, ag_sem, peer(here, offset, other))
    send_sum(tile, ag_sem, twin)

    @pl.when(s != 0)
    def _():
        late = late_tile(0, 0, s)
        settle(rbuf2.at[pl.ds(1, 63)], rs2_sem.at[1])
        out[core, late] = summed([mine[late]] + [rbuf2[slot] for slot in range(1, 64)])
        for offset in OFFSETS:
            send_sum(late, ag2_sem, peer(here, offset))

    settle(rbuf, ag_sem.at[1])
    forward = pltpu.make_async_remote_copy(
        src_ref=out.at[core, pl.ds(EARLY, 80 - EARLY)],
        dst_ref=out.at[core, pl.ds(EARLY, 80 - EARLY)],
        send_sem=fw_sem.at[0],
        recv_sem=fw_sem.at[1],
        device_id=twin,
        device_id_type=MESH,
    )
    calls = iter(range(16))

    def between():
        if next(calls) == FORWARD_AFTER:

            @pl.when(s == 0)
            def _():
                settle(rbuf2.at[pl.ds(0, 48)], ag2_sem.at[1])

            @pl.when(s != 0)
            def _():
                settle(rbuf2.at[pl.ds(0, 47)], ag2_sem.at[1])

            forward.start()

    block = load_block(out, 0, 0, total) + unit(128)
    leaf, dets[0] = invert_leaf([block[8 * i : 8 * i + 8] for i in range(16)], between)
    leaf = jnp.concatenate(leaf, axis=0)
    inverse0[...] = leaf
    side = load_block(out, 1, 0, total)
    first = dot_exact(leaf, side.T)
    first0[...] = first
    block = load_block(out, 1, 1, total) + unit(128) - dot_exact(side, first)
    leaf, dets[1] = invert_leaf([block[8 * i : 8 * i + 8] for i in range(16)], between)
    inverse1[...] = jnp.concatenate(leaf, axis=0)

    swap_early.wait_send()
    swap_late.wait_send()
    settle(rbuf, rs_sem.at[0])
    settle(rbuf, ag_sem.at[0])

    @pl.when(s == 0)
    def _():
        settle(rbuf2.at[pl.ds(0, 48)], rs2_sem.at[0])

    @pl.when(s != 0)
    def _():
        settle(rbuf2.at[pl.ds(0, 47)], rs2_sem.at[0])
        settle(rbuf, ag2_sem.at[0])

    forward.wait()


def sub_row(x, s):
    return jnp.broadcast_to(x[s : s + 1, :], (8, 128))


def lane_col(x, j):
    return jnp.broadcast_to(x[:, j : j + 1], (8, 128))


def invert_leaf(rows, between):
    lane = lax.broadcasted_iota(jnp.int32, (8, 128), 1)
    sub = lax.broadcasted_iota(jnp.int32, (8, 128), 0)
    rows = list(rows)
    dets = jnp.ones((8, 128), F32)
    zero = jnp.zeros((8, 128), F32)
    nv = GROUP // 8
    for g in range(128 // GROUP):
        a = GROUP * g
        own = [nv * g + v for v in range(nv)]
        near = [i for i in range(own[-1] + 1, own[-1] + 1 + nv) if i < 16]
        cols = [[lane_col(rows[m], a + j) for m in own] for j in range(GROUP)]
        left = {i: [lane_col(rows[i], a + j) for j in range(GROUP)] for i in near}
        inside = (lane >= a) & (lane < a + GROUP)
        top = [jnp.where(inside, (lane - a == sub + 8 * v).astype(F32), rows[m]) for v, m in enumerate(own)]
        diag, off = [zero] * nv, [zero] * nv
        for k in range(0, GROUP, 2):
            v0, s0 = divmod(k, 8)
            c0, c1 = cols[k], cols[k + 1]
            p00, p10 = sub_row(c0[v0], s0), sub_row(c0[v0], s0 + 1)
            p01, p11 = sub_row(c1[v0], s0), sub_row(c1[v0], s0 + 1)
            det = p00 * p11 - p01 * p10
            r = 1.0 / det
            dets = jnp.where(lane == a + k, det, dets)
            diag[v0] = jnp.where(sub == s0, p11 * r, jnp.where(sub == s0 + 1, p00 * r, diag[v0]))
            off[v0] = jnp.where(sub == s0, -p01 * r, jnp.where(sub == s0 + 1, -p10 * r, off[v0]))
            n0 = [c0[v] * p11 - c1[v] * p10 for v in range(nv)]
            n1 = [c1[v] * p00 - c0[v] * p01 for v in range(nv)]
            pair = (sub == s0) | (sub == s0 + 1)
            n0[v0] = jnp.where(pair, 0.0, n0[v0])
            n1[v0] = jnp.where(pair, 0.0, n1[v0])
            f0, f1 = [n * r for n in n0], [n * r for n in n1]
            for j in range(k + 2, GROUP):
                b0, b1 = sub_row(cols[j][v0], s0), sub_row(cols[j][v0], s0 + 1)
                if j < k + 4:
                    cols[j] = [cols[j][v] - (n0[v] * b0 + n1[v] * b1) * r for v in range(nv)]
                else:
                    cols[j] = [cols[j][v] - (f0[v] * b0 + f1[v] * b1) for v in range(nv)]
            b0, b1 = sub_row(top[v0], s0), sub_row(top[v0], s0 + 1)
            top = [top[v] - (f0[v] * b0 + f1[v] * b1) for v in range(nv)]
        swapped = [jnp.where(sub % 2 == 0, pltpu.roll(t, 7, 0), pltpu.roll(t, 1, 0)) for t in top]
        top = [diag[v] * top[v] + off[v] * swapped[v] for v in range(nv)]
        spread = [sub_row(top[j // 8], j % 8) for j in range(GROUP)]
        new = dict(zip(own, top))
        for i in near:
            terms = [left[i][j] * spread[j] for j in range(GROUP)]
            while len(terms) > 1:
                terms = [s + t for s, t in zip(terms[0::2], terms[1::2])]
            new[i] = jnp.where(inside, 0.0, rows[i]) - terms[0]
        padded = [jnp.zeros((a, 128), F32)] * (a > 0) + top + [jnp.zeros((128 - a - GROUP, 128), F32)] * (a + GROUP < 128)
        padded = jnp.concatenate(padded, axis=0)
        for start, stop in ((0, own[0]), (own[-1] + 1 + len(near), 16)):
            if stop > start:
                update = dot_exact(jnp.concatenate(rows[start:stop], axis=0), padded)
                for i in range(start, stop):
                    new[i] = jnp.where(inside, 0.0, rows[i]) - update[8 * (i - start) : 8 * (i - start) + 8]
        rows = [new[i] for i in range(16)]
        between()
    return rows, dets


def dot_exact(a, b):
    return jnp.dot(a, b, precision=lax.Precision.HIGHEST, preferred_element_type=F32)


def dot3(a, b):
    (ah, al), (bh, bl) = a, b
    small = jnp.dot(al, bh, preferred_element_type=F32) + jnp.dot(ah, bl, preferred_element_type=F32)
    return jnp.dot(ah, bh, preferred_element_type=F32) + small


def map_kernel(total, gram, high, low, inverse0, first0, inverse1, dets0, out_hbm, logdet, ob, zh, zl, mat, store_sem):
    rows, k = high.shape
    n = rows // CHUNK
    for i in range(k // 128):
        for j in range(i + 1):
            block = load_block(gram, i, j, total)
            if i == j:
                block = block + unit(128)
            else:
                mat[128 * j : 128 * j + 128, 128 * i : 128 * i + 128] = block.T
            mat[128 * i : 128 * i + 128, 128 * j : 128 * j + 128] = block

    half, count = k // 2, k // 128
    early = iter(range(n))
    weights = []

    def forward_chunk():
        i = next(early, None)
        if i is None:
            return
        if not weights:
            weights.extend(split(mat[:half, :]))
        span = slice(i * CHUNK, (i + 1) * CHUNK)
        d = dot3((high[span, :half], low[span, :half]), weights)
        ob[span, :half] = d[:, :half]
        zh[span, :], zl[span, :] = split((high[span, half:].astype(F32) + low[span, half:].astype(F32)) - d[:, half:])

    logs = jnp.log(dets0[0]) + jnp.log(dets0[1])
    for b in range(count):
        lo, hi = 128 * b, 128 * (b + 1)
        base = 0 if lo < half else half
        if b == 0:
            inverse = inverse0[...]
        elif b == 1:
            inverse = inverse1[...]
        else:
            leaf, dets = invert_leaf(
                [block[8 * i : 8 * i + 8] for i in range(16)], forward_chunk
            )
            logs = logs + jnp.log(dets)
            inverse = jnp.concatenate(leaf, axis=0)
        sides = {i: mat[128 * i : 128 * i + 128, lo:hi] for i in range(base // 128, count)}
        if b + 1 < count:
            first = dot_exact(inverse, mat[lo:hi, hi : hi + 128]) if b else first0[...]
            if b:
                block = mat[hi : hi + 128, hi : hi + 128] - dot_exact(sides[b + 1], first)
        parts = []
        if lo > base:
            parts.append(dot_exact(inverse, mat[lo:hi, base:lo]))
        parts.append(inverse)
        if b + 1 < count:
            parts.append(first)
        if hi + 128 < k:
            parts.append(dot_exact(inverse, mat[lo:hi, hi + 128 :]))
        top = jnp.concatenate(parts, axis=1)
        for i in sides:
            if i != b:
                update = dot_exact(sides[i], top)
                for j in sides:
                    rows_i, cols_j = slice(128 * i, 128 * i + 128), slice(128 * j, 128 * j + 128)
                    change = update[:, 128 * j - base : 128 * j - base + 128]
                    if j == b:
                        mat[rows_i, cols_j] = -change
                    else:
                        mat[rows_i, cols_j] -= change
        mat[lo:hi, base:] = top
    logdet[0, 0] = jnp.sum(logs[0:1, :]) * (1.0 / k)

    tail = split(mat[half:, half:])
    back = split(dot_exact(mat[half:, half:], mat[half:, :half]))
    stores = []
    for i in range(rows // STORE):
        span = slice(i * STORE, (i + 1) * STORE)
        z = zh[span, :], zl[span, :]
        ob[span, half:] = dot3(z, tail)
        ob[span, :half] += dot3(z, back)
        store = pltpu.make_async_copy(
            ob.at[pl.ds(i * STORE, STORE)], out_hbm.at[pl.ds(i * STORE, STORE)], store_sem.at[i]
        )
        store.start()
        stores.append(store)
    for store in stores:
        store.wait()


VMEM, HBM = pl.BlockSpec(memory_space=pltpu.VMEM), pl.BlockSpec(memory_space=pltpu.HBM)
DMA = pltpu.SemaphoreType.DMA


def gram_sum(sketch, total):
    rows, k = sketch.shape
    return pl.pallas_call(
        functools.partial(gram_kernel, total),
        out_shape=(
            jax.ShapeDtypeStruct((2, 80, 8, 128), F32),
            jax.ShapeDtypeStruct((rows, k), BF16),
            jax.ShapeDtypeStruct((rows, k), BF16),
            jax.ShapeDtypeStruct((128, 128), F32),
            jax.ShapeDtypeStruct((128, 128), F32),
            jax.ShapeDtypeStruct((128, 128), F32),
            jax.ShapeDtypeStruct((2, 8, 128), F32),
        ),
        in_specs=[HBM],
        out_specs=(VMEM,) * 7,
        scratch_shapes=[
            pltpu.VMEM((rows, k), F32),
            pltpu.VMEM((k, k), F32),
            pltpu.VMEM((k, k), F32),
            pltpu.VMEM((2, 80, 8, 128), F32),
            pltpu.VMEM((80, 8, 128), F32),
            pltpu.VMEM((80, 8, 128), F32),
            pltpu.VMEM((127, 8, 128), F32),
            DMA((rows // CHUNK,)),
        ]
        + [DMA((2,))] * 7,
        compiler_params=pltpu.CompilerParams(
            collective_id=0, has_side_effects=True, vmem_limit_bytes=VMEM_LIMIT
        ),
        name="gram_sum",
    )(pltpu.with_memory_space_constraint(sketch, pltpu.HBM))


def invert_and_map(total, gram, high, low, inverse0, first0, inverse1, dets):
    rows, k = high.shape
    return pl.pallas_call(
        functools.partial(map_kernel, total),
        out_shape=(jax.ShapeDtypeStruct((rows, k), F32), jax.ShapeDtypeStruct((1, 1), F32)),
        in_specs=[VMEM] * 7,
        out_specs=(HBM, pl.BlockSpec(memory_space=pltpu.SMEM)),
        scratch_shapes=[
            pltpu.VMEM((rows, k), F32),
            pltpu.VMEM((rows, k // 2), BF16),
            pltpu.VMEM((rows, k // 2), BF16),
            pltpu.VMEM((k, k), F32),
            DMA((rows // STORE,)),
        ],
        compiler_params=pltpu.CompilerParams(vmem_limit_bytes=VMEM_LIMIT),
        name="invert_and_map",
    )(gram, high, low, inverse0, first0, inverse1, dets)


def on_device(sketch):
    total = sketch.shape[0] * lax.axis_size("crow") * lax.axis_size("ccol")
    basis, logdet = invert_and_map(total, *gram_sum(sketch, total))
    return basis, logdet.reshape(())


def solution(mesh):
    return jax.shard_map(
        on_device,
        mesh=mesh,
        in_specs=(P(("crow", "ccol"), None),),
        out_specs=(P(("crow", "ccol"), None), P()),
        check_vma=False,
    )
```

```python
import functools

import jax
import jax.numpy as jnp
from jax import lax
from jax.experimental import pallas as pl
from jax.experimental.pallas import tpu as pltpu
from jax.sharding import PartitionSpec as P

MESH = pl.DeviceIdType.MESH
F32, BF16 = jnp.float32, jnp.bfloat16
VMEM_LIMIT = 36 * 2**20
CHUNK = 512
STORE = 256
FORWARD = 256
FORWARD_AFTER = 6


def split(x):
    high = x.astype(BF16)
    return high, (x - high.astype(F32)).astype(BF16)


def place():
    crow, ccol = lax.axis_index("crow"), lax.axis_index("ccol")
    return crow // 4, crow % 4, ccol // 2, ccol % 2


def peer(here, offset, other=False):
    z, x, y, core = here
    dz, dx, dy = offset
    return (((z + dz) % 4) * 4 + (x + dx) % 4, ((y + dy) % 4) * 2 + (1 - core if other else core))


def hops(offset):
    return sum(min(d, 4 - d) for d in offset)


OFFSETS = sorted(
    [(dz, dx, dy) for dz in range(4) for dx in range(4) for dy in range(4) if (dz, dx, dy) != (0, 0, 0)],
    key=lambda o: (-hops(o), o),
)


def opposite(offset):
    return tuple((d + 2) % 4 for d in offset)


NEAR = [o for o in OFFSETS if (hops(o), o) < (hops(opposite(o)), opposite(o))]
EARLY = 32


def early_tile(z, x, s):
    flip = 2 * (s // 2)
    return 4 * ((z + flip) % 4) + (x + flip) % 4 + 16 * (s % 2)


def block_tiles(i, j):
    start = 8 * (i * (i + 1) // 2 + j)
    return slice(start, start + 8)


def load_block(tiles_ref, i, j, total):
    tiles = block_tiles(i, j)
    return jnp.stack([tiles_ref[0, tiles], tiles_ref[1, tiles]], axis=1).reshape(128, 128) * (1.0 / total)


def unit(n):
    return (lax.broadcasted_iota(jnp.int32, (n, n), 0) == lax.broadcasted_iota(jnp.int32, (n, n), 1)).astype(F32)


def gram_kernel(
    total, x_hbm, out, high, low, inverse0, first0, third0, inverse1, dets, xb, acc, cross, part, crecv, mine, recv,
    load_sem, swap_sem, swap2_sem, rs_sem, rs2_sem, ag_sem, ag2_sem, fw_sem,
):
    rows = x_hbm.shape[0]
    rbuf, rbuf2 = recv.at[pl.ds(0, 63)], recv.at[pl.ds(63, 64)]
    n = rows // CHUNK
    loads = [
        pltpu.make_async_copy(x_hbm.at[pl.ds(i * CHUNK, CHUNK)], xb.at[pl.ds(i * CHUNK, CHUNK)], load_sem.at[i])
        for i in range(n)
    ]
    for load in loads:
        load.start()

    here = place()
    z, x, y, core = here
    s = (x + y + z) % 4
    twin = peer(here, (0, 0, 0), True)
    barrier = pltpu.get_barrier_semaphore()
    greeted = [peer(here, offset) for offset in OFFSETS]
    greeted += [peer(here, tuple((4 - d) % 4 for d in offset), True) for offset in NEAR]
    greeted.append(twin)

    def greet(devices):
        for device in devices:
            pl.semaphore_signal(barrier, inc=1, device_id=device, device_id_type=MESH)

    greet(greeted[:48])
    dims = (((0,), (0,)), ((), ()))
    for i in range(n):
        loads[i].wait()
        span = slice(i * CHUNK, (i + 1) * CHUNK)
        h, l = split(xb[span, :])
        high[span, :] = h
        low[span, :] = l
        a0 = lax.dot_general(h[:, :256], h[:, :256], dims, preferred_element_type=F32)
        a1 = lax.dot_general(h[:, 256:], h, dims, preferred_element_type=F32)
        b = lax.dot_general(h, l, dims, preferred_element_type=F32)
        if i == 0:
            acc[:256, :256] = a0
            acc[256:, :] = a1
            cross[...] = b
            greet(greeted[48:])
        else:
            acc[:256, :256] += a0
            acc[256:, :] += a1
            cross[...] += b

    def fill(blocks):
        for i, j in blocks:
            si, sj = slice(128 * i, 128 * i + 128), slice(128 * j, 128 * j + 128)
            block = (acc[si, sj] + (cross[si, sj] + cross[sj, si].T)).reshape(8, 2, 8, 128)
            for c in range(2):
                part[c, block_tiles(i, j)] = block[:, c]

    def swap(tiles, sem):
        return pltpu.make_async_remote_copy(
            src_ref=part.at[1 - core, tiles],
            dst_ref=crecv.at[tiles],
            send_sem=sem.at[0],
            recv_sem=sem.at[1],
            device_id=twin,
            device_id_type=MESH,
        )

    fill([(0, 0), (1, 0), (1, 1), (2, 0)])
    pl.semaphore_wait(barrier, len(greeted))
    swap_early, swap_late = swap(pl.ds(0, EARLY), swap_sem), swap(pl.ds(EARLY, 80 - EARLY), swap2_sem)
    swap_early.start()
    fill([(2, 1), (2, 2), (3, 0), (3, 1), (3, 2), (3, 3)])
    swap_late.start()
    swap_early.wait_recv()
    mine[:EARLY] = part[core, :EARLY] + crecv[:EARLY]
    for slot, offset in enumerate(OFFSETS):
        dz, dx, dy = offset
        pltpu.make_async_remote_copy(
            src_ref=mine.at[early_tile((z + dz) % 4, (x + dx) % 4, (s + dz + dx + dy) % 4)],
            dst_ref=rbuf.at[slot],
            send_sem=rs_sem.at[0],
            recv_sem=rs_sem.at[1],
            device_id=peer(here, offset),
            device_id_type=MESH,
        ).start()
    swap_late.wait_recv()
    mine[EARLY:] = part[core, EARLY:] + crecv[EARLY:]

    def late_tile(dz, dx, t):
        return EARLY + 3 * (4 * ((z + dz) % 4) + (x + dx) % 4) + t - 1

    def scatter_late(dz, dx, t):
        dy = (t + 12 - s - dz - dx) % 4
        return pltpu.make_async_remote_copy(
            src_ref=mine.at[late_tile(dz, dx, t)],
            dst_ref=rbuf2.at[16 * dz + 4 * dx + dy],
            send_sem=rs2_sem.at[0],
            recv_sem=rs2_sem.at[1],
            device_id=peer(here, (dz, dx, dy)),
            device_id_type=MESH,
        )

    for dz in (2, 1, 3, 0):
        for dx in (2, 1, 3, 0):
            if (dz, dx) != (0, 0):
                for t in (1, 2, 3):
                    scatter_late(dz, dx, t).start()
    for t in (1, 2, 3):

        @pl.when(s != t)
        def _():
            scatter_late(0, 0, t).start()

    def send_sum(tile, sem, device):
        pltpu.make_async_remote_copy(
            src_ref=out.at[core, tile],
            dst_ref=out.at[core, tile],
            send_sem=sem.at[0],
            recv_sem=sem.at[1],
            device_id=device,
            device_id_type=MESH,
        ).start()

    def settle(ref, sem):
        pltpu.make_async_copy(ref, ref, sem).wait()

    tile = early_tile(z, x, s)
    settle(rbuf, rs_sem.at[1])
    terms = {offset: rbuf[slot] for slot, offset in enumerate(OFFSETS)}
    terms[0, 0, 0] = mine[tile]
    out[core, tile] = tree_sum([terms[o] + terms[opposite(o)] for o in [(0, 0, 0)] + NEAR])
    for offset in NEAR:
        for other in (False, True):
            send_sum(tile, ag_sem, peer(here, offset, other))
    send_sum(tile, ag_sem, twin)

    @pl.when(s != 0)
    def _():
        late = late_tile(0, 0, s)
        settle(rbuf2.at[pl.ds(1, 63)], rs2_sem.at[1])
        out[core, late] = tree_sum([mine[late]] + [rbuf2[slot] for slot in range(1, 64)])
        for offset in OFFSETS:
            send_sum(late, ag2_sem, peer(here, offset))

    settle(rbuf, ag_sem.at[1])
    forward = pltpu.make_async_remote_copy(
        src_ref=out.at[core, pl.ds(EARLY, 80 - EARLY)],
        dst_ref=out.at[core, pl.ds(EARLY, 80 - EARLY)],
        send_sem=fw_sem.at[0],
        recv_sem=fw_sem.at[1],
        device_id=twin,
        device_id_type=MESH,
    )
    calls = iter(range(16))

    def between():
        if next(calls) == FORWARD_AFTER:

            @pl.when(s == 0)
            def _():
                settle(rbuf2.at[pl.ds(0, 48)], ag2_sem.at[1])

            @pl.when(s != 0)
            def _():
                settle(rbuf2.at[pl.ds(0, 47)], ag2_sem.at[1])

            forward.start()

    block = load_block(out, 0, 0, total) + unit(128)
    leaf, dets[0] = invert_leaf([block[8 * i : 8 * i + 8] for i in range(16)], between)
    leaf = jnp.concatenate(leaf, axis=0)
    inverse0[...] = leaf
    side = load_block(out, 1, 0, total)
    first = dot_exact(leaf, side.T)
    first0[...] = first
    third0[...] = dot_exact(leaf, load_block(out, 2, 0, total).T)
    block = load_block(out, 1, 1, total) + unit(128) - dot_exact(side, first)
    leaf, dets[1] = invert_leaf([block[8 * i : 8 * i + 8] for i in range(16)], between)
    inverse1[...] = jnp.concatenate(leaf, axis=0)

    swap_early.wait_send()
    swap_late.wait_send()
    settle(rbuf, rs_sem.at[0])
    settle(rbuf, ag_sem.at[0])

    @pl.when(s == 0)
    def _():
        settle(rbuf2.at[pl.ds(0, 48)], rs2_sem.at[0])

    @pl.when(s != 0)
    def _():
        settle(rbuf2.at[pl.ds(0, 47)], rs2_sem.at[0])
        settle(rbuf, ag2_sem.at[0])

    forward.wait()


def tree_sum(values):
    while len(values) > 1:
        values = [a + b for a, b in zip(values[0::2], values[1::2])]
    return values[0]


def sub_row(x, s):
    return jnp.broadcast_to(x[s : s + 1, :], (8, 128))


def lane_col(x, j):
    return jnp.broadcast_to(x[:, j : j + 1], (8, 128))


def invert_leaf(rows, between):
    lane = lax.broadcasted_iota(jnp.int32, (8, 128), 1)
    sub = lax.broadcasted_iota(jnp.int32, (8, 128), 0)
    rows = list(rows)
    dets = jnp.ones((8, 128), F32)

    def eliminate(a, cols, top, dets):
        nv = len(top)
        diag = off = jnp.zeros((8, 128), F32)
        for k in range(0, 8, 2):
            c0, c1 = cols[k], cols[k + 1]
            p00, p10 = sub_row(c0[0], k), sub_row(c0[0], k + 1)
            p01, p11 = sub_row(c1[0], k), sub_row(c1[0], k + 1)
            det = p00 * p11 - p01 * p10
            r = 1.0 / det
            dets = jnp.where(lane == a + k, det, dets)
            diag = jnp.where(sub == k, p11 * r, jnp.where(sub == k + 1, p00 * r, diag))
            off = jnp.where(sub == k, -p01 * r, jnp.where(sub == k + 1, -p10 * r, off))
            pair = (sub == k) | (sub == k + 1)
            n0 = [c0[v] * p11 - c1[v] * p10 for v in range(nv)]
            n1 = [c1[v] * p00 - c0[v] * p01 for v in range(nv)]
            n0[0], n1[0] = jnp.where(pair, 0.0, n0[0]), jnp.where(pair, 0.0, n1[0])
            f0, f1 = [n * r for n in n0], [n * r for n in n1]
            for j in range(k + 2, len(cols)):
                if j < 8:
                    b0, b1 = sub_row(cols[j][0], k), sub_row(cols[j][0], k + 1)
                else:
                    b0, b1 = sub_row(c0[1], j - 8), sub_row(c1[1], j - 8)
                for v in range(nv) if j < 8 else range(1, nv):
                    if j < k + 4:
                        cols[j][v] = cols[j][v] - (n0[v] * b0 + n1[v] * b1) * r
                    else:
                        cols[j][v] = cols[j][v] - (f0[v] * b0 + f1[v] * b1)
            b0, b1 = sub_row(top[0], k), sub_row(top[0], k + 1)
            top = [top[v] - (f0[v] * b0 + f1[v] * b1) for v in range(nv)]
        swapped = jnp.where(sub % 2 == 0, pltpu.roll(top[0], 7, 0), pltpu.roll(top[0], 1, 0))
        return [diag * top[0] + off * swapped] + top[1:], dets

    for g in range(8):
        a = 16 * g
        near = [2 * g + 2, 2 * g + 3] if g < 7 else []
        cols = [[lane_col(rows[2 * g + v], a + j) for v in range(2)] for j in range(8)]
        cols += [[None, lane_col(rows[2 * g + 1], a + 8 + j)] for j in range(8)]
        left = {i: [lane_col(rows[i], a + j) for j in range(16)] for i in near}
        inside, half0, half1 = (lane >= a) & (lane < a + 16), (lane >= a) & (lane < a + 8), (lane >= a + 8) & (lane < a + 16)
        top = [jnp.where(half0, (lane - a == sub).astype(F32), rows[2 * g]), jnp.where(half0, 0.0, rows[2 * g + 1])]
        (top0, top1), dets = eliminate(a, cols, top, dets)
        cross = [lane_col(top0, a + 8 + j) for j in range(8)]
        top1 = jnp.where(half1, (lane - a - 8 == sub).astype(F32), top1)
        (top1,), dets = eliminate(a + 8, [[c[1]] for c in cols[8:]], [top1], dets)
        spread = [sub_row(top1, j) for j in range(8)]
        terms = [cross[j] * spread[j] for j in range(8)]
        top0 = jnp.where(half1, 0.0, top0) - tree_sum(terms)
        spread = [sub_row(top0, j) for j in range(8)] + spread
        new = {2 * g: top0, 2 * g + 1: top1}
        for i in near:
            new[i] = jnp.where(inside, 0.0, rows[i]) - tree_sum([left[i][j] * spread[j] for j in range(16)])
        padded = [jnp.zeros((a, 128), F32)] * (a > 0) + [top0, top1] + [jnp.zeros((112 - a, 128), F32)] * (a < 112)
        padded = jnp.concatenate(padded, axis=0)
        for start, stop in ((0, 2 * g), (2 * g + 2 + len(near), 16)):
            if stop > start:
                update = dot_exact(jnp.concatenate(rows[start:stop], axis=0), padded)
                for i in range(start, stop):
                    new[i] = jnp.where(inside, 0.0, rows[i]) - update[8 * (i - start) : 8 * (i - start) + 8]
        rows = [new[i] for i in range(16)]
        between()
    return rows, dets


def dot_exact(a, b):
    return jnp.dot(a, b, precision=lax.Precision.HIGHEST, preferred_element_type=F32)


def dot3(a, b):
    (ah, al), (bh, bl) = a, b
    return jnp.dot(
        jnp.concatenate([ah, al, ah], axis=1), jnp.concatenate([bh, bh, bl], axis=0), preferred_element_type=F32
    )


def map_kernel(total, gram, high, low, inverse0, first0, third0, inverse1, dets0, out_hbm, logdet, ob, zh, zl, mat, store_sem):
    rows, k = high.shape
    for i in range(k // 128):
        for j in range(i + 1):
            block = load_block(gram, i, j, total)
            if i == j:
                block = block + unit(128)
            else:
                mat[128 * j : 128 * j + 128, 128 * i : 128 * i + 128] = block.T
            mat[128 * i : 128 * i + 128, 128 * j : 128 * j + 128] = block

    half, count = k // 2, k // 128
    early = iter(range(rows // FORWARD))
    weights = []

    def forward_chunk():
        i = next(early, None)
        if i is None:
            return
        if not weights:
            weights.extend(split(mat[:half, :]))
        span = slice(i * FORWARD, (i + 1) * FORWARD)
        d = dot3((high[span, :half], low[span, :half]), weights)
        ob[span, :half] = d[:, :half]
        zh[span, :], zl[span, :] = split((high[span, half:].astype(F32) + low[span, half:].astype(F32)) - d[:, half:])

    logs = jnp.log(dets0[0]) + jnp.log(dets0[1])
    for b in range(count):
        lo, hi = 128 * b, 128 * (b + 1)
        base = 0 if lo < half else half
        if b == 0:
            inverse = inverse0[...]
        elif b == 1:
            inverse = inverse1[...]
        else:
            leaf, dets = invert_leaf(
                [block[8 * i : 8 * i + 8] for i in range(16)], forward_chunk
            )
            logs = logs + jnp.log(dets)
            inverse = jnp.concatenate(leaf, axis=0)
        sides = {i: mat[128 * i : 128 * i + 128, lo:hi] for i in range(base // 128, count)}
        if b + 1 < count:
            first = dot_exact(inverse, mat[lo:hi, hi : hi + 128]) if b else first0[...]
            if b:
                block = mat[hi : hi + 128, hi : hi + 128] - dot_exact(sides[b + 1], first)
        parts = []
        if lo > base:
            parts.append(dot_exact(inverse, mat[lo:hi, base:lo]))
        parts.append(inverse)
        if b + 1 < count:
            parts.append(first)
        after = hi + 128
        if b == 0:
            parts.append(third0[...])
            after += 128
        if after < k:
            parts.append(dot_exact(inverse, mat[lo:hi, after:]))
        top = jnp.concatenate(parts, axis=1)
        for i in sides:
            if i != b:
                update = dot_exact(sides[i], top)
                for j in sides:
                    rows_i, cols_j = slice(128 * i, 128 * i + 128), slice(128 * j, 128 * j + 128)
                    change = update[:, 128 * j - base : 128 * j - base + 128]
                    if j == b:
                        mat[rows_i, cols_j] = -change
                    else:
                        mat[rows_i, cols_j] -= change
        mat[lo:hi, base:] = top
    logdet[0, 0] = jnp.sum(logs[0:1, :]) * (1.0 / k)

    tail = split(mat[half:, half:])
    back = split(dot_exact(mat[half:, half:], mat[half:, :half]))
    stores = []
    for i in range(rows // STORE):
        span = slice(i * STORE, (i + 1) * STORE)
        z = zh[span, :], zl[span, :]
        ob[span, half:] = dot3(z, tail)
        ob[span, :half] += dot3(z, back)
        store = pltpu.make_async_copy(
            ob.at[pl.ds(i * STORE, STORE)], out_hbm.at[pl.ds(i * STORE, STORE)], store_sem.at[i]
        )
        store.start()
        stores.append(store)
    for store in stores:
        store.wait()


VMEM, HBM = pl.BlockSpec(memory_space=pltpu.VMEM), pl.BlockSpec(memory_space=pltpu.HBM)
DMA = pltpu.SemaphoreType.DMA


def gram_sum(sketch, total):
    rows, k = sketch.shape
    return pl.pallas_call(
        functools.partial(gram_kernel, total),
        out_shape=(
            jax.ShapeDtypeStruct((2, 80, 8, 128), F32),
            jax.ShapeDtypeStruct((rows, k), BF16),
            jax.ShapeDtypeStruct((rows, k), BF16),
            jax.ShapeDtypeStruct((128, 128), F32),
            jax.ShapeDtypeStruct((128, 128), F32),
            jax.ShapeDtypeStruct((128, 128), F32),
            jax.ShapeDtypeStruct((128, 128), F32),
            jax.ShapeDtypeStruct((2, 8, 128), F32),
        ),
        in_specs=[HBM],
        out_specs=(VMEM,) * 8,
        scratch_shapes=[
            pltpu.VMEM((rows, k), F32),
            pltpu.VMEM((k, k), F32),
            pltpu.VMEM((k, k), F32),
            pltpu.VMEM((2, 80, 8, 128), F32),
            pltpu.VMEM((80, 8, 128), F32),
            pltpu.VMEM((80, 8, 128), F32),
            pltpu.VMEM((127, 8, 128), F32),
            DMA((rows // CHUNK,)),
        ]
        + [DMA((2,))] * 7,
        compiler_params=pltpu.CompilerParams(
            collective_id=0, has_side_effects=True, vmem_limit_bytes=VMEM_LIMIT
        ),
        name="gram_sum",
    )(pltpu.with_memory_space_constraint(sketch, pltpu.HBM))


def invert_and_map(total, gram, high, low, inverse0, first0, third0, inverse1, dets):
    rows, k = high.shape
    return pl.pallas_call(
        functools.partial(map_kernel, total),
        out_shape=(jax.ShapeDtypeStruct((rows, k), F32), jax.ShapeDtypeStruct((1, 1), F32)),
        in_specs=[VMEM] * 8,
        out_specs=(HBM, pl.BlockSpec(memory_space=pltpu.SMEM)),
        scratch_shapes=[
            pltpu.VMEM((rows, k), F32),
            pltpu.VMEM((rows, k // 2), BF16),
            pltpu.VMEM((rows, k // 2), BF16),
            pltpu.VMEM((k, k), F32),
            DMA((rows // STORE,)),
        ],
        compiler_params=pltpu.CompilerParams(vmem_limit_bytes=VMEM_LIMIT),
        name="invert_and_map",
    )(gram, high, low, inverse0, first0, third0, inverse1, dets)


def on_device(sketch):
    total = sketch.shape[0] * lax.axis_size("crow") * lax.axis_size("ccol")
    basis, logdet = invert_and_map(total, *gram_sum(sketch, total))
    return basis, logdet.reshape(())


def solution(mesh):
    return jax.shard_map(
        on_device,
        mesh=mesh,
        in_specs=(P(("crow", "ccol"), None),),
        out_specs=(P(("crow", "ccol"), None), P()),
        check_vma=False,
    )
```
